32 devices in a mesh: tile: 8 (over z, y), row: 4 (over x, core).
Axes of the slice: x: 2, y: 2, z: 4, core: 2. Of those that a mesh axis runs over, the one named last changes fastest.
Arguments:
- cam_disp: bfloat16 [4, 8, 4, 2, 256, 512], P('row', 'tile')
- footprint: int32 [4, 8, 2, 2], P('row', 'tile'), may hold values from 0 to 15, as said below
- stencil: int32 [4, 8, 2, 2, 2, 256], P('row', 'tile'), may hold values from 0 to 12
- frac: float32 [4, 8, 2, 2, 2, 256], P('row', 'tile'), may hold values from 0 to 1
- coef: float32 [4, 8, 2, 3, 4, 256], P('row', 'tile'), may hold values from -3 to 3
Outputs:
- velocity: bfloat16 [4, 8, 2, 3, 256, 512], P('row', 'tile')
- rfactor: float32 [512, 512], replicated
The draws below stay inside these ranges and needn't reach their ends.
Inputs may be any that keep to these rules, and one draw needn't show every extreme that they name: `footprint`: for each device, the camera tiles named for camera 0 all lie in one row group and are distinct; those for camera 1 lie in other row groups. So a device needs at most 2 distinct camera tiles from any one row group, and exactly 2 from one of them.
All inputs are finite; a program needn't handle non-finite values.
Results may differ from the reference program's by a relative error of at most 0.0015.
The reference program's roundings to bfloat16 on the way count: a program that leaves them out, or rounds other values in their place, can miss the bound.
Values may be sent and summed in bfloat16 or wider, within the bound.
A program may use at most 512 MiB of HBM per device.

```python
import jax
import jax.numpy as jnp
from jax import lax

S = 512
TILE_SIDE = 16
WT_DEV = 2
PIX = 256
WC = 256
CAM_DEV = 4
N_TILE = 8
N_ROW = 4


def draw_cam_disp(key, part):
    keys = jax.random.split(jax.random.fold_in(key, 11), 4)
    base = jax.random.normal(keys[0], (N_ROW, N_TILE, CAM_DEV, 2, PIX, 1), jnp.float32)
    scales = jnp.exp(jax.random.uniform(keys[1], (N_ROW, N_TILE, CAM_DEV, 1, 1, 1), jnp.float32, jnp.log(0.5), jnp.log(3.0)))
    noise = jax.random.normal(keys[2], (N_ROW, N_TILE, CAM_DEV, 2, PIX, S), jnp.float32)
    column = jnp.exp(jax.random.uniform(keys[3], (S,), jnp.float32, jnp.log(0.3), jnp.log(3.0)))
    mix = 0.8
    return (scales * column * (mix * base + noise)).astype(jnp.bfloat16)


def draw_footprint(key, part):
    keys = jax.random.split(jax.random.fold_in(key, 23), 4)
    owners = N_ROW * N_TILE
    first_group = jax.random.randint(keys[0], (owners, 1), 0, N_ROW)
    perm_keys = jax.random.split(keys[1], owners)
    local_first = jax.vmap(lambda k: jax.random.permutation(k, CAM_DEV)[:WT_DEV])(perm_keys)
    other = (first_group + 1 + jax.random.randint(keys[2], (owners, WT_DEV), 0, N_ROW - 1)) % N_ROW
    local_second = jax.random.randint(keys[3], (owners, WT_DEV), 0, CAM_DEV)
    first = first_group * CAM_DEV + local_first
    second = other * CAM_DEV + local_second
    both = jnp.stack([first, second], axis=-1)
    return both.reshape(N_ROW, N_TILE, WT_DEV, 2).astype(jnp.int32)


def with_ends(entries, stream_key, smallest, largest):
    longest = entries.shape.index(max(entries.shape))
    spots = []
    for shift in (0, 1):
        where = [jax.random.randint(jax.random.fold_in(stream_key, axis), (), 0, length) for axis, length in enumerate(entries.shape)]
        where[longest] = (where[longest] + shift) % entries.shape[longest]
        spots.append(tuple(where))
    return entries.at[spots[0]].set(smallest).at[spots[1]].set(largest)


def shard_levels(stream_key, extent, shards, low, high):
    level, own = 1.0, jax.random.fold_in(stream_key, 6)
    for position, blocks in shards:
        draws = jnp.exp(jax.random.uniform(jax.random.fold_in(own, position), (blocks,), jnp.float32, low / len(shards), high / len(shards)))
        level = level * jnp.repeat(draws, extent[position] // blocks).reshape([-1 if axis == position else 1 for axis in range(len(extent))])
    return level


def scatter_about(own_key, extent, spread, bound, cuts=(), kind=jnp.bfloat16):
    result = jax.random.normal(own_key, extent, jnp.float32) * spread
    if len(cuts) > 0:
        result = shard_levels(own_key, extent, cuts, -0.22, 0.18) * result
    return jnp.clip(result, min=-bound, max=bound).astype(kind)


def setup_inputs(seed: int = 0) -> dict:
    streams_of = jax.random.split(jax.random.key(seed), 6)
    return {
        "cam_disp": draw_cam_disp(jax.random.fold_in(streams_of[5], 71), 0),
        "footprint": draw_footprint(jax.random.fold_in(streams_of[5], 71), 0),
        "stencil": with_ends(jax.random.randint(streams_of[2], (N_ROW, N_TILE, WT_DEV, 2, 2, WC), 0, TILE_SIDE - 3), jax.random.fold_in(streams_of[2], 1), 0, (TILE_SIDE - 3) - 1).astype(jnp.int32),
        "frac": jnp.clip(1.0 * jax.random.uniform(streams_of[3], (N_ROW, N_TILE, WT_DEV, 2, 2, WC), jnp.float32) ** shard_levels(streams_of[3], (N_ROW, N_TILE, WT_DEV, 2, 2, WC), ((0, 4), (1, 8)), -0.2, 0.2), 0.0, 1.0),
        "coef": scatter_about(streams_of[4], (N_ROW, N_TILE, WT_DEV, 3, 4, WC), 0.5, 3.0, ((0, 4), (1, 8)), jnp.float32),
    }


def catmull(t):
    k0 = ((-0.5 * t + 1.0) * t - 0.5) * t
    k1 = (1.5 * t - 2.5) * t * t + 1.0
    k2 = ((-1.5 * t + 2.0) * t + 0.5) * t
    k3 = (0.5 * t - 0.5) * t * t
    return (k0, k1, k2, k3)

def axis_weights(base, fraction, side):
    positions = jnp.arange(side, dtype=jnp.int32)
    weights = catmull(fraction)
    total = jnp.zeros((base.shape[0], side), jnp.float32)
    for shift in range(4):
        total = total + weights[shift][:, None] * (positions[None, :] == base[:, None] + shift).astype(jnp.float32)
    return total

def interp_matrix(base_pair, frac_pair, side):
    rows = axis_weights(base_pair[0], frac_pair[0], side)
    cols = axis_weights(base_pair[1], frac_pair[1], side)
    whole = rows[:, :, None] * cols[:, None, :]
    return whole.reshape(whole.shape[0], side * side).astype(jnp.bfloat16)

def velocity_tiles(pool, ids, sten, fraction, weights_coef):
    world = weights_coef.shape[0]
    cells = weights_coef.shape[3]
    picked = jnp.take(pool, ids.reshape(-1), axis=0)
    mats = jax.vmap(lambda b, f: interp_matrix(b, f, TILE_SIDE))(sten.reshape(world * 2, 2, cells), fraction.reshape(world * 2, 2, cells))
    interp = jnp.einsum('pqx,pjxs->pjqs', mats.astype(jnp.float32), picked.astype(jnp.float32))
    interp = interp.reshape(world, 4, cells, interp.shape[-1])
    total = jnp.zeros((world, 3, cells, interp.shape[-1]), jnp.float32)
    for inner in range(4):
        total = total + weights_coef[:, :, inner, :, None] * interp[:, None, inner]
    return total.astype(jnp.bfloat16)

def reference(cam_disp, footprint, stencil, frac, coef):
    groups = footprint.shape[0]
    columns = footprint.shape[1]
    snaps = cam_disp.shape[-1]

    def one_device(index):
        grp = (index // columns).astype(jnp.int32)
        col = (index % columns).astype(jnp.int32)
        pool = jnp.take(cam_disp, col, axis=1)
        pool = pool.reshape(groups * cam_disp.shape[2], 2, cam_disp.shape[4], snaps)
        ids = footprint[grp, col]
        vel = velocity_tiles(pool, ids, stencil[grp, col], frac[grp, col], coef[grp, col])
        rows = vel.reshape(-1, snaps)
        gram = jnp.dot(rows.T.astype(jnp.float32), rows.astype(jnp.float32), preferred_element_type=jnp.float32)
        return (vel, gram)
    vels, grams = lax.map(one_device, jnp.arange(groups * columns, dtype=jnp.int32))
    velocity = vels.reshape(footprint.shape[:3] + vels.shape[2:])
    total_rows = groups * columns * vels.shape[1] * 3 * vels.shape[3]
    gram = jnp.sum(grams, axis=0) / jnp.float32(total_rows)
    rfactor = jnp.linalg.cholesky(gram).T
    return (velocity, rfactor)
```

```python
import functools

import jax
import jax.numpy as jnp
from jax import lax
from jax.experimental import pallas as pl
from jax.experimental.pallas import tpu as pltpu
from jax.sharding import PartitionSpec as P

TILE_SIDE = 16
BLK = 128
SUB = 8
MESH = pl.DeviceIdType.MESH
VMEM_LIMIT = 48 * 1024 * 1024


def flip(index, bit):
    return index + bit - 2 * bit * (lax.rem(index // bit, 2))


def exchange_kernel(n, count, cam_ref, pool_ref, send_sem, recv_sem, own_sem):
    me = lax.axis_index("row")
    bits = [1 << k for k in range(n.bit_length() - 1)]
    barrier = pltpu.get_barrier_semaphore()
    for bit in bits:
        pl.semaphore_signal(barrier, inc=1, device_id={"row": flip(me, bit)}, device_id_type=MESH)
    pl.semaphore_wait(barrier, len(bits))

    def copy_of(slot, bit, tile):
        src = cam_ref.at[tile] if slot == 0 else pool_ref.at[slot, tile]
        return pltpu.make_async_remote_copy(
            src_ref=src,
            dst_ref=pool_ref.at[slot + bit, tile],
            send_sem=send_sem.at[slot + bit, tile],
            recv_sem=recv_sem.at[slot + bit, tile],
            device_id={"row": flip(me, bit)},
            device_id_type=MESH,
        )

    started = []
    for tile in range(count):
        for bit in reversed(bits):
            c = copy_of(0, bit, tile)
            c.start()
            started.append(c)
    own = pltpu.make_async_copy(cam_ref, pool_ref.at[0], own_sem)
    own.start()
    arrived = set()
    for slot in sorted(range(2, n), key=lambda d: -(d & -d)):
        low = slot & -slot
        if low == 1:
            continue
        for tile in range(count):
            copy_of(slot - low, low, tile).wait_recv()
            arrived.add((slot, tile))
            for bit in bits:
                if bit < low:
                    c = copy_of(slot, bit, tile)
                    c.start()
                    started.append(c)
    for slot in range(1, n):
        low = slot & -slot
        for tile in range(count):
            if (slot, tile) not in arrived:
                copy_of(slot - low, low, tile).wait_recv()
    for c in started:
        c.wait_send()
    own.wait()


def exchange(tiles, n):
    count = tiles.shape[0]
    return pl.pallas_call(
        functools.partial(exchange_kernel, n, count),
        out_shape=jax.ShapeDtypeStruct((n,) + tiles.shape, tiles.dtype),
        in_specs=[pl.BlockSpec(memory_space=pl.ANY)],
        out_specs=pl.BlockSpec(memory_space=pl.ANY),
        scratch_shapes=[
            pltpu.SemaphoreType.DMA((n, count)),
            pltpu.SemaphoreType.DMA((n, count)),
            pltpu.SemaphoreType.DMA,
        ],
        compiler_params=pltpu.CompilerParams(collective_id=0, has_side_effects=True),
        name="camera_exchange",
    )(tiles)


def catmull(t):
    k0 = ((-0.5 * t + 1.0) * t - 0.5) * t
    k1 = (1.5 * t - 2.5) * t * t + 1.0
    k2 = ((-1.5 * t + 2.0) * t + 0.5) * t
    k3 = (0.5 * t - 0.5) * t * t
    return (k0, k1, k2, k3)


def spread(base, weights, positions):
    total = jnp.zeros(positions.shape, jnp.float32)
    for shift in range(4):
        total = jnp.where(positions == base + shift, weights[shift], total)
    return total


def velocity_kernel(ids_ref, *refs):
    first_ref, second_ref, sten_ref, frac_ref, coef_ref, vel_ref, gram_ref = refs
    pix = first_ref.shape[-2]
    snaps = first_ref.shape[-1]
    cells = sten_ref.shape[-1]
    pixel = lax.broadcasted_iota(jnp.int32, (pix, cells), 0)
    prow, pcol = pixel // TILE_SIDE, pixel % TILE_SIDE
    coef = coef_ref[0].T
    interp = []
    for c, tile_ref in enumerate((first_ref, second_ref)):
        sten = sten_ref[0, c]
        frac = frac_ref[0, c]
        rows = spread(sten[0:1], catmull(frac[0:1]), prow)
        cols = spread(sten[1:2], catmull(frac[1:2]), pcol)
        mat = (rows * cols).astype(jnp.bfloat16)
        for j in range(2):
            interp.append(
                lax.dot_general(
                    mat, tile_ref[0, 0, j], (((0,), (0,)), ((), ())), preferred_element_type=jnp.float32
                )
            )
    for k in range(3):
        total = coef[:, 4 * k : 4 * k + 1] * interp[0]
        for i in range(1, 4):
            total = total + coef[:, 4 * k + i : 4 * k + i + 1] * interp[i]
        vel_ref[0, k] = total.astype(jnp.bfloat16)
    rows = vel_ref[0].reshape(3 * cells, snaps)

    @pl.when(pl.program_id(0) == 0)
    def _():
        gram_ref[...] = jnp.zeros_like(gram_ref)

    offset = 0
    for ib in range(snaps // BLK):
        lo = ib * BLK
        width = snaps - lo
        part = lax.dot_general(
            rows[:, lo : lo + BLK], rows[:, lo:], (((0,), (0,)), ((), ())), preferred_element_type=jnp.float32
        )
        for jb in range(width // BLK):
            gram_ref[offset : offset + BLK] += part[:, jb * BLK : (jb + 1) * BLK]
            offset += BLK


def velocity_and_gram(pool, slots, stencil, frac, coef):
    n, count, two, pix, snaps = pool.shape
    world, cells = coef.shape[0], coef.shape[-1]
    nb = snaps // BLK
    packed = nb * (nb + 1) // 2 * BLK

    def tile_spec(c):
        return pl.BlockSpec(
            (1, 1, two, pix, snaps),
            lambda w, ids: (ids[2 * w + c] // count, ids[2 * w + c] % count, 0, 0, 0),
        )

    return pl.pallas_call(
        velocity_kernel,
        grid_spec=pltpu.PrefetchScalarGridSpec(
            num_scalar_prefetch=1,
            grid=(world,),
            in_specs=[
                tile_spec(0),
                tile_spec(1),
                pl.BlockSpec((1, 2, 2, cells), lambda w, ids: (w, 0, 0, 0)),
                pl.BlockSpec((1, 2, 2, cells), lambda w, ids: (w, 0, 0, 0)),
                pl.BlockSpec((1, 12, cells), lambda w, ids: (w, 0, 0)),
            ],
            out_specs=[
                pl.BlockSpec((1, 3, cells, snaps), lambda w, ids: (w, 0, 0, 0)),
                pl.BlockSpec((packed, BLK), lambda w, ids: (0, 0)),
            ],
        ),
        out_shape=[
            jax.ShapeDtypeStruct((world, 3, cells, snaps), jnp.bfloat16),
            jax.ShapeDtypeStruct((packed, BLK), jnp.float32),
        ],
        compiler_params=pltpu.CompilerParams(vmem_limit_bytes=VMEM_LIMIT),
        name="velocity_gram",
    )(slots, pool, pool, stencil, frac, coef.reshape(world, 12, cells))


def sum_phases(rows, n_row, n_tile):
    phases = []
    for size in (2, n_row // 2 * 2, n_tile // 2):
        cut = rows % (size * SUB) == 0
        phases.append((size, rows, cut))
        rows = rows // size if cut else rows
    return phases


def sum_kernel(phases, g_ref, out_ref, acc, *scratch):
    row, tile = lax.axis_index("row"), lax.axis_index("tile")
    row_low, row_high = lax.rem(row, 2), row // 2
    tile_low, tile_high = lax.rem(tile, 2), tile // 2
    ranks = (row_low, row_high * 2 + tile_low, tile_high)
    recv = scratch[: len(phases)]
    send_sem, recv_sem = scratch[len(phases) :]

    def device(phase, rank):
        if phase == 0:
            return (tile, row_high * 2 + rank)
        if phase == 1:
            return (tile_high * 2 + lax.rem(rank, 2), rank // 2 * 2 + row_low)
        return (rank * 2 + tile_low, row)

    barrier = pltpu.get_barrier_semaphore()
    total = 0
    for p, (size, _, _) in enumerate(phases):
        for step in range(1, size):
            peer = lax.rem(ranks[p] + step, size)
            pl.semaphore_signal(barrier, inc=1, device_id=device(p, peer), device_id_type=MESH)
            total += 1
    pl.semaphore_wait(barrier, total)

    sem = 0
    start = 0
    src = g_ref
    starts = []
    for p, (size, rows, cut) in enumerate(phases):
        starts.append(start)
        piece = rows // size if cut else rows
        copies = []
        for step in range(1, size):
            peer = lax.rem(ranks[p] + step, size)
            lo = start + peer * piece if cut else start
            copies.append(
                pltpu.make_async_remote_copy(
                    src_ref=src.at[pl.ds(pl.multiple_of(lo, SUB), piece)],
                    dst_ref=recv[p].at[step - 1],
                    send_sem=send_sem.at[sem],
                    recv_sem=recv_sem.at[sem],
                    device_id=device(p, peer),
                    device_id_type=MESH,
                )
            )
            sem += 1
        for c in copies:
            c.start()
        for c in copies:
            c.wait()
        start = start + ranks[p] * piece if cut else start
        where = pl.ds(pl.multiple_of(start, SUB), piece)
        if cut:
            value = src[where]
            for step in range(1, size):
                value = value + recv[p][step - 1]
        else:
            value = jnp.zeros((piece, BLK), jnp.float32)
            for source in range(size):
                mine = (ranks[p] == source).astype(jnp.float32)
                value = value + src[where] * mine
                for step in range(1, size):
                    theirs = (lax.rem(ranks[p] - step + size, size) == source).astype(jnp.float32)
                    value = value + recv[p][step - 1] * theirs
        last = p == len(phases) - 1
        target = out_ref if last else acc
        target[where] = value
        src = acc

    for p in reversed(range(len(phases))):
        size, rows, cut = phases[p]
        if not cut:
            continue
        piece = rows // size
        where = pl.ds(pl.multiple_of(starts[p] + ranks[p] * piece, SUB), piece)
        copies = []
        for step in range(1, size):
            peer = lax.rem(ranks[p] + step, size)
            copies.append(
                pltpu.make_async_remote_copy(
                    src_ref=out_ref.at[where],
                    dst_ref=out_ref.at[where],
                    send_sem=send_sem.at[sem],
                    recv_sem=recv_sem.at[sem],
                    device_id=device(p, peer),
                    device_id_type=MESH,
                )
            )
            sem += 1
        for c in copies:
            c.start()
        for step, c in enumerate(copies, 1):
            c.wait()


def sum_all(gram, n_row, n_tile):
    phases = sum_phases(gram.shape[0], n_row, n_tile)
    sems = 2 * sum(size - 1 for size, _, _ in phases)
    return pl.pallas_call(
        functools.partial(sum_kernel, phases),
        out_shape=jax.ShapeDtypeStruct(gram.shape, gram.dtype),
        in_specs=[pl.BlockSpec(memory_space=pltpu.VMEM)],
        out_specs=pl.BlockSpec(memory_space=pltpu.VMEM),
        scratch_shapes=[pltpu.VMEM(gram.shape, gram.dtype)]
        + [
            pltpu.VMEM((size - 1, rows // size if cut else rows, BLK), gram.dtype)
            for size, rows, cut in phases
        ]
        + [pltpu.SemaphoreType.DMA((sems,)), pltpu.SemaphoreType.DMA((sems,))],
        compiler_params=pltpu.CompilerParams(
            collective_id=1, has_side_effects=True, vmem_limit_bytes=VMEM_LIMIT
        ),
        name="gram_sum",
    )(gram)


def row_of(x, k):
    return jnp.broadcast_to(x[k : k + 1], x.shape)


def eliminate(panel, out_ref, base, low, step, width):
    r0 = pl.multiple_of(step * SUB, SUB)
    sub = lax.broadcasted_iota(jnp.int32, (SUB, BLK), 0)
    lane = lax.broadcasted_iota(jnp.int32, (SUB, BLK), 1)
    picks = [jnp.full((SUB, BLK), 0, jnp.int32) + (r0 + j) for j in range(SUB)]

    def columns(x):
        return [jnp.take_along_axis(x, picks[j], axis=1, mode="promise_in_bounds") for j in range(SUB)]

    rows = [panel[pl.ds(r0, SUB), b * BLK : (b + 1) * BLK] for b in range(width)]
    cols = columns(rows[0])
    scale = jnp.zeros((SUB, BLK), jnp.float32)
    inverses, heads, tails = [], [], []
    for k in range(SUB):
        root = lax.rsqrt(row_of(cols[k], k))
        inverse = root * root
        scale = jnp.where(sub == k, root, scale)
        head = {j: row_of(cols[j], k) for j in range(k + 1, SUB)}
        tail = [row_of(x, k) for x in rows]
        factor = jnp.where(sub > k, cols[k] * inverse, 0.0)
        for j in range(k + 1, SUB):
            cols[j] = cols[j] - factor * head[j]
        rows = [x - factor * y for x, y in zip(rows, tail)]
        inverses.append(inverse)
        heads.append(head)
        tails.append(tail)
    for b in range(width):
        done = rows[b] * scale
        if b == 0:
            done = jnp.where(lane >= sub + r0, done, 0.0)
        out_ref[pl.ds(pl.multiple_of(base + r0, SUB), SUB), base + b * BLK : base + (b + 1) * BLK] = done
    for i in range(low, BLK // SUB):
        here = pl.ds(i * SUB, SUB)
        other = [panel[here, b * BLK : (b + 1) * BLK] for b in range(width)]
        cols = columns(other[0])
        for k in range(SUB):
            factor = cols[k] * inverses[k]
            for j in range(k + 1, SUB):
                cols[j] = cols[j] - factor * heads[k][j]
            other = [x - factor * y for x, y in zip(other, tails[k])]
        for b in range(width):
            panel[here, b * BLK : (b + 1) * BLK] = other[b]


def factor_kernel(scaling, g_ref, out_ref, *panels):
    nb = len(panels)
    out_ref[...] = jnp.zeros_like(out_ref)
    offset = 0
    for ib in range(nb):
        for jb in range(nb - ib):
            panels[ib][:, jb * BLK : (jb + 1) * BLK] = g_ref[offset : offset + BLK] * scaling
            offset += BLK
    steps = BLK // SUB
    part = 4
    for ib in range(nb):
        base = ib * BLK
        width = nb - ib
        for low in range(0, steps, part):

            def body(step, carry, low=low):
                eliminate(panels[ib], out_ref, base, low, step, width)
                return carry

            lax.fori_loop(low, low + part, body, 0)
        for jb in range(ib + 1, nb):
            left = out_ref[base : base + BLK, jb * BLK : (jb + 1) * BLK]
            right = out_ref[base : base + BLK, jb * BLK :]
            panels[jb][...] -= lax.dot_general(
                left,
                right,
                (((0,), (0,)), ((), ())),
                precision=lax.Precision.HIGHEST,
                preferred_element_type=jnp.float32,
            )


def factor(gram, snaps, total_rows):
    nb = snaps // BLK
    return pl.pallas_call(
        functools.partial(factor_kernel, 1.0 / total_rows),
        out_shape=jax.ShapeDtypeStruct((snaps, snaps), jnp.float32),
        in_specs=[pl.BlockSpec(memory_space=pltpu.VMEM)],
        out_specs=pl.BlockSpec(memory_space=pltpu.VMEM),
        scratch_shapes=[pltpu.VMEM((BLK, (nb - ib) * BLK), jnp.float32) for ib in range(nb)],
        compiler_params=pltpu.CompilerParams(vmem_limit_bytes=VMEM_LIMIT),
        name="cholesky_factor",
    )(gram)


def local(n_row, n_tile, cam_disp, footprint, stencil, frac, coef):
    count, two, pix, snaps = cam_disp.shape[2:]
    world, cells = footprint.shape[2], coef.shape[-1]
    pool = exchange(cam_disp.reshape(count, two, pix, snaps), n_row)
    ids = footprint.reshape(world * 2)
    slots = jnp.bitwise_xor(ids // count, lax.axis_index("row")) * count + ids % count
    velocity, gram = velocity_and_gram(
        pool,
        slots,
        stencil.reshape(world, 2, 2, cells),
        frac.reshape(world, 2, 2, cells),
        coef.reshape(world, 3, 4, cells),
    )
    rfactor = factor(sum_all(gram, n_row, n_tile), snaps, n_row * n_tile * world * 3 * cells)
    return (velocity.reshape(1, 1, world, 3, cells, snaps), rfactor)


def solution(mesh):
    in_specs = (
        P("row", "tile", None, None, None, None),
        P("row", "tile", None, None),
        P("row", "tile", None, None, None, None),
        P("row", "tile", None, None, None, None),
        P("row", "tile", None, None, None, None),
    )
    out_specs = (P("row", "tile", None, None, None, None), P())
    body = functools.partial(local, mesh.shape["row"], mesh.shape["tile"])
    return jax.shard_map(body, mesh=mesh, in_specs=in_specs, out_specs=out_specs, check_vma=False)
```

```python
import functools

import jax
import jax.numpy as jnp
from jax import lax
from jax.experimental import pallas as pl
from jax.experimental.pallas import tpu as pltpu
from jax.sharding import PartitionSpec as P

TILE_SIDE = 16
BLK = 128
SUB = 8
MESH = pl.DeviceIdType.MESH
VMEM_LIMIT = 48 * 1024 * 1024


def flip(index, bit):
    return index + bit - 2 * bit * (lax.rem(index // bit, 2))


def exchange_kernel(n, cam_ref, ids_ref, pool_ref, cams, mine, asked, wanted, staged, sems, foot_send, foot_recv, send, recv):
    _, _, count, two, pix, snaps = cam_ref.shape
    world = pool_ref.shape[0]
    me = lax.axis_index("row")

    def peer(d):
        index = me
        for k in range(n.bit_length() - 1):
            if d >> k & 1:
                index = flip(index, 1 << k)
        return {"row": index}

    load = pltpu.make_async_copy(cam_ref.at[0, 0], cams, sems.at[0])
    load.start()
    line = lax.broadcasted_iota(jnp.int32, mine.shape, 0)
    filled = jnp.zeros(mine.shape, jnp.int32)
    for i in range(2 * world):
        filled = jnp.where(line == i, ids_ref[0, 0, i // 2, i % 2], filled)
    mine[...] = filled
    asked[0] = filled
    barrier = pltpu.get_barrier_semaphore()
    for d in range(1, n):
        pl.semaphore_signal(barrier, inc=1, device_id=peer(d), device_id_type=MESH)
    pl.semaphore_wait(barrier, n - 1)

    requests = [
        pltpu.make_async_remote_copy(
            src_ref=mine,
            dst_ref=asked.at[d],
            send_sem=foot_send.at[d],
            recv_sem=foot_recv.at[d],
            device_id=peer(d),
            device_id_type=MESH,
        )
        for d in range(1, n)
    ]
    for r in requests:
        r.start()
    for r in requests:
        r.wait()
    known = pltpu.make_async_copy(asked, wanted, sems.at[1])
    known.start()
    known.wait()
    load.wait()

    copies = []
    order = sorted(range(n), key=lambda d: -d)
    for w in range(world):
        for d in order:
            first, second = wanted[d, 2 * w, 0], wanted[d, 2 * w + 1, 0]
            here = jnp.where(first // count == me, first % count, second % count)
            staged[w, d] = cams[here]
            if d == 0:
                c = pltpu.make_async_copy(staged.at[w, 0], pool_ref.at[w, 0], sems.at[2 + w])
            else:
                c = pltpu.make_async_remote_copy(
                    src_ref=staged.at[w, d],
                    dst_ref=pool_ref.at[w, d],
                    send_sem=send.at[w, d],
                    recv_sem=recv.at[w, d],
                    device_id=peer(d),
                    device_id_type=MESH,
                )
            c.start()
            copies.append(c)
    for c in copies:
        c.wait()


def exchange(cam_disp, footprint, n):
    _, _, count, two, pix, snaps = cam_disp.shape
    world = footprint.shape[2]
    lines = -(-2 * world // SUB) * SUB
    tile = (two, pix, snaps)
    return pl.pallas_call(
        functools.partial(exchange_kernel, n),
        out_shape=jax.ShapeDtypeStruct((world, n) + tile, cam_disp.dtype),
        in_specs=[pl.BlockSpec(memory_space=pl.ANY), pl.BlockSpec(memory_space=pltpu.SMEM)],
        out_specs=pl.BlockSpec(memory_space=pl.ANY),
        scratch_shapes=[
            pltpu.VMEM((count,) + tile, cam_disp.dtype),
            pltpu.VMEM((lines, BLK), jnp.int32),
            pltpu.VMEM((n, lines, BLK), jnp.int32),
            pltpu.SMEM((n, lines, BLK), jnp.int32),
            pltpu.VMEM((world, n) + tile, cam_disp.dtype),
            pltpu.SemaphoreType.DMA((2 + world,)),
            pltpu.SemaphoreType.DMA((n,)),
            pltpu.SemaphoreType.DMA((n,)),
            pltpu.SemaphoreType.DMA((world, n)),
            pltpu.SemaphoreType.DMA((world, n)),
        ],
        compiler_params=pltpu.CompilerParams(
            collective_id=0, has_side_effects=True, vmem_limit_bytes=VMEM_LIMIT
        ),
        name="camera_exchange",
    )(cam_disp, footprint)


def catmull(t):
    k0 = ((-0.5 * t + 1.0) * t - 0.5) * t
    k1 = (1.5 * t - 2.5) * t * t + 1.0
    k2 = ((-1.5 * t + 2.0) * t + 0.5) * t
    k3 = (0.5 * t - 0.5) * t * t
    return (k0, k1, k2, k3)


def spread(base, weights, positions):
    total = jnp.zeros(positions.shape, jnp.float32)
    for shift in range(4):
        total = jnp.where(positions == base + shift, weights[shift], total)
    return total


def velocity_kernel(ids_ref, me_ref, *refs):
    first_ref, second_ref, sten_ref, frac_ref, coef_ref, vel_ref, gram_ref = refs
    pix = first_ref.shape[-2]
    snaps = first_ref.shape[-1]
    cells = sten_ref.shape[-1]
    pixel = lax.broadcasted_iota(jnp.int32, (pix, cells), 0)
    prow, pcol = pixel // TILE_SIDE, pixel % TILE_SIDE
    interp = []
    for c, tile_ref in enumerate((first_ref, second_ref)):
        sten = sten_ref[0, 0, 0, c]
        frac = frac_ref[0, 0, 0, c]
        rows = spread(sten[0:1], catmull(frac[0:1]), prow)
        cols = spread(sten[1:2], catmull(frac[1:2]), pcol)
        mat = (rows * cols).astype(jnp.bfloat16)
        for j in range(2):
            interp.append(
                lax.dot_general(
                    mat, tile_ref[0, 0, j], (((0,), (0,)), ((), ())), preferred_element_type=jnp.float32
                )
            )
    for k in range(3):
        coef = coef_ref[0, 0, 0, k].T
        total = coef[:, 0:1] * interp[0]
        for i in range(1, 4):
            total = total + coef[:, i : i + 1] * interp[i]
        vel_ref[0, k] = total.astype(jnp.bfloat16)
    rows = vel_ref[0].reshape(3 * cells, snaps)

    @pl.when(pl.program_id(0) == 0)
    def _():
        gram_ref[...] = jnp.zeros_like(gram_ref)

    offset = 0
    for ib in range(snaps // BLK):
        lo = ib * BLK
        width = snaps - lo
        part = lax.dot_general(
            rows[:, lo : lo + BLK], rows[:, lo:], (((0,), (0,)), ((), ())), preferred_element_type=jnp.float32
        )
        for jb in range(width // BLK):
            gram_ref[offset : offset + BLK] += part[:, jb * BLK : (jb + 1) * BLK]
            offset += BLK


def velocity_and_gram(pool, count, footprint, stencil, frac, coef):
    _, _, two, pix, snaps = pool.shape
    world, cells = footprint.shape[2], coef.shape[-1]
    nb = snaps // BLK
    packed = nb * (nb + 1) // 2 * BLK

    def tile_spec(c):
        return pl.BlockSpec(
            (1, 1, two, pix, snaps),
            lambda w, ids, me: (w, (ids[0, 0, w, c] // count) ^ me[0], 0, 0, 0),
        )

    return pl.pallas_call(
        velocity_kernel,
        grid_spec=pltpu.PrefetchScalarGridSpec(
            num_scalar_prefetch=2,
            grid=(world,),
            in_specs=[
                tile_spec(0),
                tile_spec(1),
                pl.BlockSpec((1, 1, 1, 2, 2, cells), lambda w, ids, me: (0, 0, w, 0, 0, 0)),
                pl.BlockSpec((1, 1, 1, 2, 2, cells), lambda w, ids, me: (0, 0, w, 0, 0, 0)),
                pl.BlockSpec((1, 1, 1, 3, 4, cells), lambda w, ids, me: (0, 0, w, 0, 0, 0)),
            ],
            out_specs=[
                pl.BlockSpec((1, 3, cells, snaps), lambda w, ids, me: (w, 0, 0, 0)),
                pl.BlockSpec((packed, BLK), lambda w, ids, me: (0, 0)),
            ],
        ),
        out_shape=[
            jax.ShapeDtypeStruct((world, 3, cells, snaps), jnp.bfloat16),
            jax.ShapeDtypeStruct((packed, BLK), jnp.float32),
        ],
        compiler_params=pltpu.CompilerParams(vmem_limit_bytes=VMEM_LIMIT),
        name="velocity_gram",
    )(footprint, lax.axis_index("row").reshape(1), pool, pool, stencil, frac, coef)


def sum_phases(rows, n_row, n_tile):
    phases = []
    for size in (2, n_row // 2 * 2, n_tile // 2):
        cut = rows % (size * SUB) == 0
        phases.append((size, rows, cut))
        rows = rows // size if cut else rows
    return phases


def sum_kernel(phases, g_ref, out_ref, acc, *scratch):
    row, tile = lax.axis_index("row"), lax.axis_index("tile")
    row_low, row_high = lax.rem(row, 2), row // 2
    tile_low, tile_high = lax.rem(tile, 2), tile // 2
    ranks = (row_low, row_high * 2 + tile_low, tile_high)
    recv = scratch[: len(phases)]
    send_sem, recv_sem = scratch[len(phases) :]

    def device(phase, rank):
        if phase == 0:
            return (tile, row_high * 2 + rank)
        if phase == 1:
            return (tile_high * 2 + lax.rem(rank, 2), rank // 2 * 2 + row_low)
        return (rank * 2 + tile_low, row)

    barrier = pltpu.get_barrier_semaphore()
    total = 0
    for p, (size, _, _) in enumerate(phases):
        for step in range(1, size):
            peer = lax.rem(ranks[p] + step, size)
            pl.semaphore_signal(barrier, inc=1, device_id=device(p, peer), device_id_type=MESH)
            total += 1
    pl.semaphore_wait(barrier, total)

    sem = 0
    start = 0
    src = g_ref
    starts = []
    for p, (size, rows, cut) in enumerate(phases):
        starts.append(start)
        piece = rows // size if cut else rows
        copies = []
        for step in range(1, size):
            peer = lax.rem(ranks[p] + step, size)
            lo = start + peer * piece if cut else start
            copies.append(
                pltpu.make_async_remote_copy(
                    src_ref=src.at[pl.ds(pl.multiple_of(lo, SUB), piece)],
                    dst_ref=recv[p].at[step - 1],
                    send_sem=send_sem.at[sem],
                    recv_sem=recv_sem.at[sem],
                    device_id=device(p, peer),
                    device_id_type=MESH,
                )
            )
            sem += 1
        for c in copies:
            c.start()
        for c in copies:
            c.wait()
        start = start + ranks[p] * piece if cut else start
        where = pl.ds(pl.multiple_of(start, SUB), piece)
        if cut:
            value = src[where]
            for step in range(1, size):
                value = value + recv[p][step - 1]
        else:
            value = jnp.zeros((piece, BLK), jnp.float32)
            for source in range(size):
                mine = (ranks[p] == source).astype(jnp.float32)
                value = value + src[where] * mine
                for step in range(1, size):
                    theirs = (lax.rem(ranks[p] - step + size, size) == source).astype(jnp.float32)
                    value = value + recv[p][step - 1] * theirs
        last = p == len(phases) - 1
        target = out_ref if last else acc
        target[where] = value
        src = acc

    for p in reversed(range(len(phases))):
        size, rows, cut = phases[p]
        if not cut:
            continue
        piece = rows // size
        where = pl.ds(pl.multiple_of(starts[p] + ranks[p] * piece, SUB), piece)
        copies = []
        for step in range(1, size):
            peer = lax.rem(ranks[p] + step, size)
            copies.append(
                pltpu.make_async_remote_copy(
                    src_ref=out_ref.at[where],
                    dst_ref=out_ref.at[where],
                    send_sem=send_sem.at[sem],
                    recv_sem=recv_sem.at[sem],
                    device_id=device(p, peer),
                    device_id_type=MESH,
                )
            )
            sem += 1
        for c in copies:
            c.start()
        for step, c in enumerate(copies, 1):
            c.wait()


def sum_all(gram, n_row, n_tile):
    phases = sum_phases(gram.shape[0], n_row, n_tile)
    sems = 2 * sum(size - 1 for size, _, _ in phases)
    return pl.pallas_call(
        functools.partial(sum_kernel, phases),
        out_shape=jax.ShapeDtypeStruct(gram.shape, gram.dtype),
        in_specs=[pl.BlockSpec(memory_space=pltpu.VMEM)],
        out_specs=pl.BlockSpec(memory_space=pltpu.VMEM),
        scratch_shapes=[pltpu.VMEM(gram.shape, gram.dtype)]
        + [
            pltpu.VMEM((size - 1, rows // size if cut else rows, BLK), gram.dtype)
            for size, rows, cut in phases
        ]
        + [pltpu.SemaphoreType.DMA((sems,)), pltpu.SemaphoreType.DMA((sems,))],
        compiler_params=pltpu.CompilerParams(
            collective_id=1, has_side_effects=True, vmem_limit_bytes=VMEM_LIMIT
        ),
        name="gram_sum",
    )(gram)


def row_of(x, k):
    return jnp.broadcast_to(x[k : k + 1], x.shape)


def eliminate(panel, out_ref, base, low, step, width):
    r0 = pl.multiple_of(step * SUB, SUB)
    sub = lax.broadcasted_iota(jnp.int32, (SUB, BLK), 0)
    lane = lax.broadcasted_iota(jnp.int32, (SUB, BLK), 1)
    picks = [jnp.full((SUB, BLK), 0, jnp.int32) + (r0 + j) for j in range(SUB)]

    def columns(x):
        return [jnp.take_along_axis(x, picks[j], axis=1, mode="promise_in_bounds") for j in range(SUB)]

    rows = [panel[pl.ds(r0, SUB), b * BLK : (b + 1) * BLK] for b in range(width)]
    cols = columns(rows[0])
    scale = jnp.zeros((SUB, BLK), jnp.float32)
    inverses, heads, tails = [], [], []
    for k in range(SUB):
        root = lax.rsqrt(row_of(cols[k], k))
        inverse = root * root
        scale = jnp.where(sub == k, root, scale)
        head = {j: row_of(cols[j], k) for j in range(k + 1, SUB)}
        tail = [row_of(x, k) for x in rows]
        factor = jnp.where(sub > k, cols[k] * inverse, 0.0)
        for j in range(k + 1, SUB):
            cols[j] = cols[j] - factor * head[j]
        rows = [x - factor * y for x, y in zip(rows, tail)]
        inverses.append(inverse)
        heads.append(head)
        tails.append(tail)
    for b in range(width):
        done = rows[b] * scale
        if b == 0:
            done = jnp.where(lane >= sub + r0, done, 0.0)
        out_ref[pl.ds(pl.multiple_of(base + r0, SUB), SUB), base + b * BLK : base + (b + 1) * BLK] = done
    for i in range(low, BLK // SUB):
        here = pl.ds(i * SUB, SUB)
        other = [panel[here, b * BLK : (b + 1) * BLK] for b in range(width)]
        cols = columns(other[0])
        for k in range(SUB):
            factor = cols[k] * inverses[k]
            for j in range(k + 1, SUB):
                cols[j] = cols[j] - factor * heads[k][j]
            other = [x - factor * y for x, y in zip(other, tails[k])]
        for b in range(width):
            panel[here, b * BLK : (b + 1) * BLK] = other[b]


def factor_kernel(scaling, g_ref, out_ref, *panels):
    nb = len(panels)
    out_ref[...] = jnp.zeros_like(out_ref)
    offset = 0
    for ib in range(nb):
        for jb in range(nb - ib):
            panels[ib][:, jb * BLK : (jb + 1) * BLK] = g_ref[offset : offset + BLK] * scaling
            offset += BLK
    steps = BLK // SUB
    part = 4
    for ib in range(nb):
        base = ib * BLK
        width = nb - ib
        for low in range(0, steps, part):

            def body(step, carry, low=low):
                eliminate(panels[ib], out_ref, base, low, step, width)
                return carry

            lax.fori_loop(low, low + part, body, 0)
        for jb in range(ib + 1, nb):
            left = out_ref[base : base + BLK, jb * BLK : (jb + 1) * BLK]
            right = out_ref[base : base + BLK, jb * BLK :]
            panels[jb][...] -= lax.dot_general(
                left,
                right,
                (((0,), (0,)), ((), ())),
                precision=lax.Precision.HIGHEST,
                preferred_element_type=jnp.float32,
            )


def factor(gram, snaps, total_rows):
    nb = snaps // BLK
    return pl.pallas_call(
        functools.partial(factor_kernel, 1.0 / total_rows),
        out_shape=jax.ShapeDtypeStruct((snaps, snaps), jnp.float32),
        in_specs=[pl.BlockSpec(memory_space=pltpu.VMEM)],
        out_specs=pl.BlockSpec(memory_space=pltpu.VMEM),
        scratch_shapes=[pltpu.VMEM((BLK, (nb - ib) * BLK), jnp.float32) for ib in range(nb)],
        compiler_params=pltpu.CompilerParams(vmem_limit_bytes=VMEM_LIMIT),
        name="cholesky_factor",
    )(gram)


def local(n_row, n_tile, cam_disp, footprint, stencil, frac, coef):
    count, _, _, snaps = cam_disp.shape[2:]
    world, cells = footprint.shape[2], coef.shape[-1]
    pool = exchange(cam_disp, footprint, n_row)
    velocity, gram = velocity_and_gram(pool, count, footprint, stencil, frac, coef)
    rfactor = factor(sum_all(gram, n_row, n_tile), snaps, n_row * n_tile * world * 3 * cells)
    return (velocity.reshape(1, 1, world, 3, cells, snaps), rfactor)


def solution(mesh):
    in_specs = (
        P("row", "tile", None, None, None, None),
        P("row", "tile", None, None),
        P("row", "tile", None, None, None, None),
        P("row", "tile", None, None, None, None),
        P("row", "tile", None, None, None, None),
    )
    out_specs = (P("row", "tile", None, None, None, None), P())
    body = functools.partial(local, mesh.shape["row"], mesh.shape["tile"])
    return jax.shard_map(body, mesh=mesh, in_specs=in_specs, out_specs=out_specs, check_vma=False)
```

```python
import functools

import jax
import jax.numpy as jnp
from jax import lax
from jax.experimental import pallas as pl
from jax.experimental.pallas import tpu as pltpu
from jax.sharding import PartitionSpec as P

TILE_SIDE = 16
BLK = 128
SUB = 8
MESH = pl.DeviceIdType.MESH
VMEM_LIMIT = 48 * 1024 * 1024


def flip(index, bit):
    return index + bit - 2 * bit * (lax.rem(index // bit, 2))


def exchange_kernel(n, cam_ref, ids_ref, pool_ref, cams, mine, asked, wanted, staged, sems, foot_send, foot_recv, send, recv):
    _, _, count, two, pix, snaps = cam_ref.shape
    world = pool_ref.shape[0]
    me = lax.axis_index("row")

    def peer(d):
        index = me
        for k in range(n.bit_length() - 1):
            if d >> k & 1:
                index = flip(index, 1 << k)
        return {"row": index}

    load = pltpu.make_async_copy(cam_ref.at[0, 0], cams, sems.at[0])
    load.start()
    line = lax.broadcasted_iota(jnp.int32, mine.shape, 0)
    filled = jnp.zeros(mine.shape, jnp.int32)
    for i in range(2 * world):
        filled = jnp.where(line == i, ids_ref[0, 0, i // 2, i % 2], filled)
    mine[...] = filled
    asked[0] = filled
    barrier = pltpu.get_barrier_semaphore()
    for d in range(1, n):
        pl.semaphore_signal(barrier, inc=1, device_id=peer(d), device_id_type=MESH)
    pl.semaphore_wait(barrier, n - 1)

    requests = [
        pltpu.make_async_remote_copy(
            src_ref=mine,
            dst_ref=asked.at[d],
            send_sem=foot_send.at[d],
            recv_sem=foot_recv.at[d],
            device_id=peer(d),
            device_id_type=MESH,
        )
        for d in range(1, n)
    ]
    for r in requests:
        r.start()
    for r in requests:
        r.wait()
    known = pltpu.make_async_copy(asked, wanted, sems.at[1])
    known.start()
    known.wait()
    load.wait()

    copies = []
    order = sorted(range(n), key=lambda d: -d)
    for w in range(world):
        for d in order:
            first, second = wanted[d, 2 * w, 0], wanted[d, 2 * w + 1, 0]
            here = jnp.where(first // count == me, first % count, second % count)
            staged[w, d] = cams[here]
            if d == 0:
                c = pltpu.make_async_copy(staged.at[w, 0], pool_ref.at[w, 0], sems.at[2 + w])
            else:
                c = pltpu.make_async_remote_copy(
                    src_ref=staged.at[w, d],
                    dst_ref=pool_ref.at[w, d],
                    send_sem=send.at[w, d],
                    recv_sem=recv.at[w, d],
                    device_id=peer(d),
                    device_id_type=MESH,
                )
            c.start()
            copies.append(c)
    for c in copies:
        c.wait()


def exchange(cam_disp, footprint, n):
    _, _, count, two, pix, snaps = cam_disp.shape
    world = footprint.shape[2]
    lines = -(-2 * world // SUB) * SUB
    tile = (two, pix, snaps)
    return pl.pallas_call(
        functools.partial(exchange_kernel, n),
        out_shape=jax.ShapeDtypeStruct((world, n) + tile, cam_disp.dtype),
        in_specs=[pl.BlockSpec(memory_space=pl.ANY), pl.BlockSpec(memory_space=pltpu.SMEM)],
        out_specs=pl.BlockSpec(memory_space=pl.ANY),
        scratch_shapes=[
            pltpu.VMEM((count,) + tile, cam_disp.dtype),
            pltpu.VMEM((lines, BLK), jnp.int32),
            pltpu.VMEM((n, lines, BLK), jnp.int32),
            pltpu.SMEM((n, lines, BLK), jnp.int32),
            pltpu.VMEM((world, n) + tile, cam_disp.dtype),
            pltpu.SemaphoreType.DMA((2 + world,)),
            pltpu.SemaphoreType.DMA((n,)),
            pltpu.SemaphoreType.DMA((n,)),
            pltpu.SemaphoreType.DMA((world, n)),
            pltpu.SemaphoreType.DMA((world, n)),
        ],
        compiler_params=pltpu.CompilerParams(
            collective_id=0, has_side_effects=True, vmem_limit_bytes=VMEM_LIMIT
        ),
        name="camera_exchange",
    )(cam_disp, footprint)


def catmull(t):
    k0 = ((-0.5 * t + 1.0) * t - 0.5) * t
    k1 = (1.5 * t - 2.5) * t * t + 1.0
    k2 = ((-1.5 * t + 2.0) * t + 0.5) * t
    k3 = (0.5 * t - 0.5) * t * t
    return (k0, k1, k2, k3)


def spread(base, weights, positions):
    total = jnp.zeros(positions.shape, jnp.float32)
    for shift in range(4):
        total = jnp.where(positions == base + shift, weights[shift], total)
    return total


def velocity_kernel(ids_ref, me_ref, *refs):
    first_ref, second_ref, sten_ref, frac_ref, coef_ref, vel_ref, gram_ref = refs
    pix = first_ref.shape[-2]
    snaps = first_ref.shape[-1]
    cells = sten_ref.shape[-1]
    pixel = lax.broadcasted_iota(jnp.int32, (pix, cells), 0)
    prow, pcol = pixel // TILE_SIDE, pixel % TILE_SIDE
    interp = []
    for c, tile_ref in enumerate((first_ref, second_ref)):
        sten = sten_ref[0, 0, 0, c]
        frac = frac_ref[0, 0, 0, c]
        rows = spread(sten[0:1], catmull(frac[0:1]), prow)
        cols = spread(sten[1:2], catmull(frac[1:2]), pcol)
        mat = (rows * cols).astype(jnp.bfloat16)
        for j in range(2):
            interp.append(
                lax.dot_general(
                    mat, tile_ref[0, 0, j], (((0,), (0,)), ((), ())), preferred_element_type=jnp.float32
                )
            )
    for k in range(3):
        coef = coef_ref[0, 0, 0, k].T
        total = coef[:, 0:1] * interp[0]
        for i in range(1, 4):
            total = total + coef[:, i : i + 1] * interp[i]
        vel_ref[0, k] = total.astype(jnp.bfloat16)
    rows = vel_ref[0].reshape(3 * cells, snaps)

    @pl.when(pl.program_id(0) == 0)
    def _():
        gram_ref[...] = jnp.zeros_like(gram_ref)

    offset = 0
    for ib in range(snaps // BLK):
        lo = ib * BLK
        width = snaps - lo
        part = lax.dot_general(
            rows[:, lo : lo + BLK], rows[:, lo:], (((0,), (0,)), ((), ())), preferred_element_type=jnp.float32
        )
        for jb in range(width // BLK):
            gram_ref[offset : offset + BLK] += part[:, jb * BLK : (jb + 1) * BLK]
            offset += BLK


def velocity_and_gram(pool, count, footprint, stencil, frac, coef):
    _, _, two, pix, snaps = pool.shape
    world, cells = footprint.shape[2], coef.shape[-1]
    nb = snaps // BLK
    packed = nb * (nb + 1) // 2 * BLK

    def tile_spec(c):
        return pl.BlockSpec(
            (1, 1, two, pix, snaps),
            lambda w, ids, me: (w, (ids[0, 0, w, c] // count) ^ me[0], 0, 0, 0),
        )

    return pl.pallas_call(
        velocity_kernel,
        grid_spec=pltpu.PrefetchScalarGridSpec(
            num_scalar_prefetch=2,
            grid=(world,),
            in_specs=[
                tile_spec(0),
                tile_spec(1),
                pl.BlockSpec((1, 1, 1, 2, 2, cells), lambda w, ids, me: (0, 0, w, 0, 0, 0)),
                pl.BlockSpec((1, 1, 1, 2, 2, cells), lambda w, ids, me: (0, 0, w, 0, 0, 0)),
                pl.BlockSpec((1, 1, 1, 3, 4, cells), lambda w, ids, me: (0, 0, w, 0, 0, 0)),
            ],
            out_specs=[
                pl.BlockSpec((1, 3, cells, snaps), lambda w, ids, me: (w, 0, 0, 0)),
                pl.BlockSpec((packed, BLK), lambda w, ids, me: (0, 0)),
            ],
        ),
        out_shape=[
            jax.ShapeDtypeStruct((world, 3, cells, snaps), jnp.bfloat16),
            jax.ShapeDtypeStruct((packed, BLK), jnp.float32),
        ],
        compiler_params=pltpu.CompilerParams(vmem_limit_bytes=VMEM_LIMIT),
        name="velocity_gram",
    )(footprint, lax.axis_index("row").reshape(1), pool, pool, stencil, frac, coef)


def sum_phases(rows, n_row, n_tile):
    phases = []
    for size in (2, n_row // 2 * 2, n_tile // 2):
        cut = rows % (size * SUB) == 0
        phases.append((size, rows, cut))
        rows = rows // size if cut else rows
    return phases


def sum_kernel(phases, g_ref, out_ref, acc, *scratch):
    row, tile = lax.axis_index("row"), lax.axis_index("tile")
    row_low, row_high = lax.rem(row, 2), row // 2
    tile_low, tile_high = lax.rem(tile, 2), tile // 2
    ranks = (row_low, row_high * 2 + tile_low, tile_high)
    recv = scratch[: len(phases)]
    send_sem, recv_sem = scratch[len(phases) :]

    def device(phase, rank):
        if phase == 0:
            return (tile, row_high * 2 + rank)
        if phase == 1:
            return (tile_high * 2 + lax.rem(rank, 2), rank // 2 * 2 + row_low)
        return (rank * 2 + tile_low, row)

    barrier = pltpu.get_barrier_semaphore()
    total = 0
    for p, (size, _, _) in enumerate(phases):
        for step in range(1, size):
            peer = lax.rem(ranks[p] + step, size)
            pl.semaphore_signal(barrier, inc=1, device_id=device(p, peer), device_id_type=MESH)
            total += 1
    pl.semaphore_wait(barrier, total)

    sem = 0
    start = 0
    src = g_ref
    starts = []
    for p, (size, rows, cut) in enumerate(phases):
        starts.append(start)
        piece = rows // size if cut else rows
        copies = []
        for step in range(1, size):
            peer = lax.rem(ranks[p] + step, size)
            lo = start + peer * piece if cut else start
            copies.append(
                pltpu.make_async_remote_copy(
                    src_ref=src.at[pl.ds(pl.multiple_of(lo, SUB), piece)],
                    dst_ref=recv[p].at[step - 1],
                    send_sem=send_sem.at[sem],
                    recv_sem=recv_sem.at[sem],
                    device_id=device(p, peer),
                    device_id_type=MESH,
                )
            )
            sem += 1
        for c in copies:
            c.start()
        for c in copies:
            c.wait()
        start = start + ranks[p] * piece if cut else start
        where = pl.ds(pl.multiple_of(start, SUB), piece)
        if cut:
            value = src[where]
            for step in range(1, size):
                value = value + recv[p][step - 1]
        else:
            value = jnp.zeros((piece, BLK), jnp.float32)
            for source in range(size):
                mine = (ranks[p] == source).astype(jnp.float32)
                value = value + src[where] * mine
                for step in range(1, size):
                    theirs = (lax.rem(ranks[p] - step + size, size) == source).astype(jnp.float32)
                    value = value + recv[p][step - 1] * theirs
        last = p == len(phases) - 1
        target = out_ref if last else acc
        target[where] = value
        src = acc

    for p in reversed(range(len(phases))):
        size, rows, cut = phases[p]
        if not cut:
            continue
        piece = rows // size
        where = pl.ds(pl.multiple_of(starts[p] + ranks[p] * piece, SUB), piece)
        copies = []
        for step in range(1, size):
            peer = lax.rem(ranks[p] + step, size)
            copies.append(
                pltpu.make_async_remote_copy(
                    src_ref=out_ref.at[where],
                    dst_ref=out_ref.at[where],
                    send_sem=send_sem.at[sem],
                    recv_sem=recv_sem.at[sem],
                    device_id=device(p, peer),
                    device_id_type=MESH,
                )
            )
            sem += 1
        for c in copies:
            c.start()
        for step, c in enumerate(copies, 1):
            c.wait()


def sum_all(gram, n_row, n_tile):
    phases = sum_phases(gram.shape[0], n_row, n_tile)
    sems = 2 * sum(size - 1 for size, _, _ in phases)
    return pl.pallas_call(
        functools.partial(sum_kernel, phases),
        out_shape=jax.ShapeDtypeStruct(gram.shape, gram.dtype),
        in_specs=[pl.BlockSpec(memory_space=pltpu.VMEM)],
        out_specs=pl.BlockSpec(memory_space=pltpu.VMEM),
        scratch_shapes=[pltpu.VMEM(gram.shape, gram.dtype)]
        + [
            pltpu.VMEM((size - 1, rows // size if cut else rows, BLK), gram.dtype)
            for size, rows, cut in phases
        ]
        + [pltpu.SemaphoreType.DMA((sems,)), pltpu.SemaphoreType.DMA((sems,))],
        compiler_params=pltpu.CompilerParams(
            collective_id=1, has_side_effects=True, vmem_limit_bytes=VMEM_LIMIT
        ),
        name="gram_sum",
    )(gram)


def row_of(x, k):
    return jnp.broadcast_to(x[k : k + 1], x.shape)


def columns(x, r0):
    return [jnp.broadcast_to(x[:, r0 + j : r0 + j + 1], x.shape) for j in range(SUB)]


def eliminate(panel, out_ref, base, step, width, rows):
    r0 = step * SUB
    sub = lax.broadcasted_iota(jnp.int32, (SUB, BLK), 0)
    lane = lax.broadcasted_iota(jnp.int32, (SUB, BLK), 1)
    cols = columns(rows[0], r0)
    scale = jnp.zeros((SUB, BLK), jnp.float32)
    inverses, heads, tails = [], [], []
    for k in range(SUB):
        root = lax.rsqrt(row_of(cols[k], k))
        inverse = root * root
        scale = jnp.where(sub == k, root, scale)
        head = {j: row_of(cols[j], k) for j in range(k + 1, SUB)}
        tail = [row_of(x, k) for x in rows]
        factor = jnp.where(sub > k, cols[k] * inverse, 0.0)
        for j in range(k + 1, SUB):
            cols[j] = cols[j] - factor * head[j]
        rows = [x - factor * y for x, y in zip(rows, tail)]
        inverses.append(inverse)
        heads.append(head)
        tails.append(tail)
    for b in range(width):
        done = rows[b] * scale
        if b == 0:
            done = jnp.where(lane >= sub + r0, done, 0.0)
        out_ref[base + r0 : base + r0 + SUB, base + b * BLK : base + (b + 1) * BLK] = done
    following = None
    for i in range(step + 1, BLK // SUB):
        here = slice(i * SUB, (i + 1) * SUB)
        other = [panel[here, b * BLK : (b + 1) * BLK] for b in range(width)]
        cols = columns(other[0], r0)
        for k in range(SUB):
            factor = cols[k] * inverses[k]
            for j in range(k + 1, SUB):
                cols[j] = cols[j] - factor * heads[k][j]
            other = [x - factor * y for x, y in zip(other, tails[k])]
        if following is None:
            following = other
        else:
            for b in range(width):
                panel[here, b * BLK : (b + 1) * BLK] = other[b]
    return following


def factor_kernel(scaling, g_ref, out_ref, *panels):
    nb = len(panels)
    out_ref[...] = jnp.zeros_like(out_ref)
    offset = 0
    for ib in range(nb):
        for jb in range(nb - ib):
            panels[ib][:, jb * BLK : (jb + 1) * BLK] = g_ref[offset : offset + BLK] * scaling
            offset += BLK
    for ib in range(nb):
        base = ib * BLK
        width = nb - ib
        rows = [panels[ib][0:SUB, b * BLK : (b + 1) * BLK] for b in range(width)]
        for step in range(BLK // SUB):
            rows = eliminate(panels[ib], out_ref, base, step, width, rows)
        for jb in range(ib + 1, nb):
            left = out_ref[base : base + BLK, jb * BLK : (jb + 1) * BLK]
            right = out_ref[base : base + BLK, jb * BLK :]
            panels[jb][...] -= lax.dot_general(
                left,
                right,
                (((0,), (0,)), ((), ())),
                precision=lax.Precision.HIGHEST,
                preferred_element_type=jnp.float32,
            )


def factor(gram, snaps, total_rows):
    nb = snaps // BLK
    return pl.pallas_call(
        functools.partial(factor_kernel, 1.0 / total_rows),
        out_shape=jax.ShapeDtypeStruct((snaps, snaps), jnp.float32),
        in_specs=[pl.BlockSpec(memory_space=pltpu.VMEM)],
        out_specs=pl.BlockSpec(memory_space=pltpu.VMEM),
        scratch_shapes=[pltpu.VMEM((BLK, (nb - ib) * BLK), jnp.float32) for ib in range(nb)],
        compiler_params=pltpu.CompilerParams(vmem_limit_bytes=VMEM_LIMIT),
        name="cholesky_factor",
    )(gram)


def local(n_row, n_tile, cam_disp, footprint, stencil, frac, coef):
    count, _, _, snaps = cam_disp.shape[2:]
    world, cells = footprint.shape[2], coef.shape[-1]
    pool = exchange(cam_disp, footprint, n_row)
    velocity, gram = velocity_and_gram(pool, count, footprint, stencil, frac, coef)
    rfactor = factor(sum_all(gram, n_row, n_tile), snaps, n_row * n_tile * world * 3 * cells)
    return (velocity.reshape(1, 1, world, 3, cells, snaps), rfactor)


def solution(mesh):
    in_specs = (
        P("row", "tile", None, None, None, None),
        P("row", "tile", None, None),
        P("row", "tile", None, None, None, None),
        P("row", "tile", None, None, None, None),
        P("row", "tile", None, None, None, None),
    )
    out_specs = (P("row", "tile", None, None, None, None), P())
    body = functools.partial(local, mesh.shape["row"], mesh.shape["tile"])
    return jax.shard_map(body, mesh=mesh, in_specs=in_specs, out_specs=out_specs, check_vma=False)
```

```python
import functools

import jax
import jax.numpy as jnp
from jax import lax
from jax.experimental import pallas as pl
from jax.experimental.pallas import tpu as pltpu
from jax.sharding import PartitionSpec as P

TILE_SIDE = 16
BLK = 128
SUB = 8
MESH = pl.DeviceIdType.MESH
VMEM_LIMIT = 48 * 1024 * 1024
VMEM_MOST = 60 * 1024 * 1024


def flip(index, bit):
    return index + bit - 2 * bit * (lax.rem(index // bit, 2))


def velocity_kernel(n, cam_ref, ids_ref, sten_ref, frac_ref, coef_ref, vel_ref, gram_ref, *scratch):
    _, _, count, two, pix, snaps = cam_ref.shape
    world = vel_ref.shape[0]
    pools = scratch[:world]
    cams, mats, mine, asked, wanted, staged, sems, foot_send, foot_recv, send, recv = scratch[world:]
    me = lax.axis_index("row")

    def peer(d):
        index = me
        for k in range(n.bit_length() - 1):
            if d >> k & 1:
                index = flip(index, 1 << k)
        return {"row": index}

    load = pltpu.make_async_copy(cam_ref.at[0, 0], cams, sems.at[0])
    load.start()
    line = lax.broadcasted_iota(jnp.int32, mine.shape, 0)
    filled = jnp.zeros(mine.shape, jnp.int32)
    for i in range(2 * world):
        filled = jnp.where(line == i, ids_ref[0, 0, i // 2, i % 2], filled)
    mine[...] = filled
    asked[0] = filled
    barrier = pltpu.get_barrier_semaphore()
    for d in range(1, n):
        pl.semaphore_signal(barrier, inc=1, device_id=peer(d), device_id_type=MESH)
    pl.semaphore_wait(barrier, n - 1)

    requests = [
        pltpu.make_async_remote_copy(
            src_ref=mine,
            dst_ref=asked.at[d],
            send_sem=foot_send.at[d],
            recv_sem=foot_recv.at[d],
            device_id=peer(d),
            device_id_type=MESH,
        )
        for d in range(1, n)
    ]
    for r in requests:
        r.start()
    for r in requests:
        r.wait()
    known = pltpu.make_async_copy(asked, wanted, sems.at[1])
    known.start()
    known.wait()
    load.wait()

    copies = []
    order = sorted(range(n), key=lambda d: -d)
    for w in range(world):
        for d in order:
            first, second = wanted[d, 2 * w, 0], wanted[d, 2 * w + 1, 0]
            here = jnp.where(first // count == me, first % count, second % count)
            if d == 0:
                pools[w][0] = cams[here]
                continue
            staged[w, d] = cams[here]
            c = pltpu.make_async_remote_copy(
                src_ref=staged.at[w, d],
                dst_ref=pools[w].at[d],
                send_sem=send.at[w, d],
                recv_sem=recv.at[w, d],
                device_id=peer(d),
                device_id_type=MESH,
            )
            c.start()
            copies.append((w, c))
    for w in range(world):
        for c in range(2):
            mats[2 * w + c] = interp_matrix(sten_ref[0, 0, w, c], frac_ref[0, 0, w, c], pix)
    gram_ref[...] = jnp.zeros_like(gram_ref)
    for w in range(world):
        for owner, c in copies:
            if owner == w:
                c.wait_recv()
        tiles = []
        for c in range(2):
            group = ids_ref[0, 0, w, c] // count
            slot = 0
            for k in range(n.bit_length() - 1):
                bit = 1 << k
                slot = slot + bit * lax.rem(group // bit + me // bit, 2)
            tiles.append(pools[w][slot])
        velocity_of(w, mats, tiles, coef_ref, vel_ref, gram_ref)
    for _, c in copies:
        c.wait_send()


def catmull(t):
    k0 = ((-0.5 * t + 1.0) * t - 0.5) * t
    k1 = (1.5 * t - 2.5) * t * t + 1.0
    k2 = ((-1.5 * t + 2.0) * t + 0.5) * t
    k3 = (0.5 * t - 0.5) * t * t
    return (k0, k1, k2, k3)


def spread(base, weights, positions):
    total = jnp.zeros(positions.shape, jnp.float32)
    for shift in range(4):
        total = jnp.where(positions == base + shift, weights[shift], total)
    return total


def interp_matrix(sten, frac, pix):
    pixel = lax.broadcasted_iota(jnp.int32, (pix, sten.shape[-1]), 0)
    rows = spread(sten[0:1], catmull(frac[0:1]), pixel // TILE_SIDE)
    cols = spread(sten[1:2], catmull(frac[1:2]), pixel % TILE_SIDE)
    return (rows * cols).astype(jnp.bfloat16)


def velocity_of(w, mats, tiles, coef_ref, vel_ref, gram_ref):
    _, _, cells, snaps = vel_ref.shape
    interp = [
        lax.dot_general(
            mats[2 * w + c], tiles[c][j], (((0,), (0,)), ((), ())), preferred_element_type=jnp.float32
        )
        for c in range(2)
        for j in range(2)
    ]
    for k in range(3):
        coef = coef_ref[0, 0, w, k].T
        total = coef[:, 0:1] * interp[0]
        for i in range(1, 4):
            total = total + coef[:, i : i + 1] * interp[i]
        vel_ref[w, k] = total.astype(jnp.bfloat16)
    rows = vel_ref[w].reshape(3 * cells, snaps)
    offset = 0
    for ib in range(snaps // BLK):
        lo = ib * BLK
        width = snaps - lo
        part = lax.dot_general(
            rows[:, lo : lo + BLK], rows[:, lo:], (((0,), (0,)), ((), ())), preferred_element_type=jnp.float32
        )
        for jb in range(width // BLK):
            gram_ref[offset : offset + BLK] += part[:, jb * BLK : (jb + 1) * BLK]
            offset += BLK


def velocity_and_gram(cam_disp, footprint, stencil, frac, coef, n):
    _, _, count, two, pix, snaps = cam_disp.shape
    world, cells = footprint.shape[2], coef.shape[-1]
    nb = snaps // BLK
    packed = nb * (nb + 1) // 2 * BLK
    lines = -(-2 * world // SUB) * SUB
    tile = (two, pix, snaps)
    vmem = pl.BlockSpec(memory_space=pltpu.VMEM)
    return pl.pallas_call(
        functools.partial(velocity_kernel, n),
        out_shape=[
            jax.ShapeDtypeStruct((world, 3, cells, snaps), jnp.bfloat16),
            jax.ShapeDtypeStruct((packed, BLK), jnp.float32),
        ],
        in_specs=[
            pl.BlockSpec(memory_space=pl.ANY),
            pl.BlockSpec(memory_space=pltpu.SMEM),
            vmem,
            vmem,
            vmem,
        ],
        out_specs=[vmem, vmem],
        scratch_shapes=[pltpu.VMEM((n,) + tile, cam_disp.dtype) for _ in range(world)]
        + [
            pltpu.VMEM((count,) + tile, cam_disp.dtype),
            pltpu.VMEM((2 * world, pix, cells), jnp.bfloat16),
            pltpu.VMEM((lines, BLK), jnp.int32),
            pltpu.VMEM((n, lines, BLK), jnp.int32),
            pltpu.SMEM((n, lines, BLK), jnp.int32),
            pltpu.VMEM((world, n) + tile, cam_disp.dtype),
            pltpu.SemaphoreType.DMA((2,)),
            pltpu.SemaphoreType.DMA((n,)),
            pltpu.SemaphoreType.DMA((n,)),
            pltpu.SemaphoreType.DMA((world, n)),
            pltpu.SemaphoreType.DMA((world, n)),
        ],
        compiler_params=pltpu.CompilerParams(
            collective_id=0, has_side_effects=True, vmem_limit_bytes=VMEM_MOST
        ),
        name="velocity_gram",
    )(cam_disp, footprint, stencil, frac, coef)


def sum_phases(rows, n_row, n_tile):
    phases = []
    for size in (2, n_row // 2 * 2, n_tile // 2):
        cut = rows % (size * SUB) == 0
        phases.append((size, rows, cut))
        rows = rows // size if cut else rows
    return phases


def sum_kernel(phases, g_ref, out_ref, acc, *scratch):
    row, tile = lax.axis_index("row"), lax.axis_index("tile")
    row_low, row_high = lax.rem(row, 2), row // 2
    tile_low, tile_high = lax.rem(tile, 2), tile // 2
    ranks = (row_low, row_high * 2 + tile_low, tile_high)
    recv = scratch[: len(phases)]
    send_sem, recv_sem = scratch[len(phases) :]

    def device(phase, rank):
        if phase == 0:
            return (tile, row_high * 2 + rank)
        if phase == 1:
            return (tile_high * 2 + lax.rem(rank, 2), rank // 2 * 2 + row_low)
        return (rank * 2 + tile_low, row)

    barrier = pltpu.get_barrier_semaphore()
    total = 0
    for p, (size, _, _) in enumerate(phases):
        for step in range(1, size):
            peer = lax.rem(ranks[p] + step, size)
            pl.semaphore_signal(barrier, inc=1, device_id=device(p, peer), device_id_type=MESH)
            total += 1
    pl.semaphore_wait(barrier, total)

    sem = 0
    start = 0
    src = g_ref
    starts = []
    for p, (size, rows, cut) in enumerate(phases):
        starts.append(start)
        piece = rows // size if cut else rows
        copies = []
        for step in range(1, size):
            peer = lax.rem(ranks[p] + step, size)
            lo = start + peer * piece if cut else start
            copies.append(
                pltpu.make_async_remote_copy(
                    src_ref=src.at[pl.ds(pl.multiple_of(lo, SUB), piece)],
                    dst_ref=recv[p].at[step - 1],
                    send_sem=send_sem.at[sem],
                    recv_sem=recv_sem.at[sem],
                    device_id=device(p, peer),
                    device_id_type=MESH,
                )
            )
            sem += 1
        for c in copies:
            c.start()
        for c in copies:
            c.wait()
        start = start + ranks[p] * piece if cut else start
        where = pl.ds(pl.multiple_of(start, SUB), piece)
        if cut:
            value = src[where]
            for step in range(1, size):
                value = value + recv[p][step - 1]
        else:
            value = jnp.zeros((piece, BLK), jnp.float32)
            for source in range(size):
                mine = (ranks[p] == source).astype(jnp.float32)
                value = value + src[where] * mine
                for step in range(1, size):
                    theirs = (lax.rem(ranks[p] - step + size, size) == source).astype(jnp.float32)
                    value = value + recv[p][step - 1] * theirs
        last = p == len(phases) - 1
        target = out_ref if last else acc
        target[where] = value
        src = acc

    for p in reversed(range(len(phases))):
        size, rows, cut = phases[p]
        if not cut:
            continue
        piece = rows // size
        where = pl.ds(pl.multiple_of(starts[p] + ranks[p] * piece, SUB), piece)
        copies = []
        for step in range(1, size):
            peer = lax.rem(ranks[p] + step, size)
            copies.append(
                pltpu.make_async_remote_copy(
                    src_ref=out_ref.at[where],
                    dst_ref=out_ref.at[where],
                    send_sem=send_sem.at[sem],
                    recv_sem=recv_sem.at[sem],
                    device_id=device(p, peer),
                    device_id_type=MESH,
                )
            )
            sem += 1
        for c in copies:
            c.start()
        for step, c in enumerate(copies, 1):
            c.wait()


def sum_all(gram, n_row, n_tile):
    phases = sum_phases(gram.shape[0], n_row, n_tile)
    sems = 2 * sum(size - 1 for size, _, _ in phases)
    return pl.pallas_call(
        functools.partial(sum_kernel, phases),
        out_shape=jax.ShapeDtypeStruct(gram.shape, gram.dtype),
        in_specs=[pl.BlockSpec(memory_space=pltpu.VMEM)],
        out_specs=pl.BlockSpec(memory_space=pltpu.VMEM),
        scratch_shapes=[pltpu.VMEM(gram.shape, gram.dtype)]
        + [
            pltpu.VMEM((size - 1, rows // size if cut else rows, BLK), gram.dtype)
            for size, rows, cut in phases
        ]
        + [pltpu.SemaphoreType.DMA((sems,)), pltpu.SemaphoreType.DMA((sems,))],
        compiler_params=pltpu.CompilerParams(
            collective_id=1, has_side_effects=True, vmem_limit_bytes=VMEM_LIMIT
        ),
        name="gram_sum",
    )(gram)


def row_of(x, k):
    return jnp.broadcast_to(x[k : k + 1], x.shape)


def columns(x, r0):
    return [jnp.broadcast_to(x[:, r0 + j : r0 + j + 1], x.shape) for j in range(SUB)]


def eliminate(panel, out_ref, base, step, width, rows):
    r0 = step * SUB
    sub = lax.broadcasted_iota(jnp.int32, (SUB, BLK), 0)
    lane = lax.broadcasted_iota(jnp.int32, (SUB, BLK), 1)
    cols = columns(rows[0], r0)
    scale = jnp.zeros((SUB, BLK), jnp.float32)
    inverses, heads, tails = [], [], []
    for k in range(SUB):
        root = lax.rsqrt(row_of(cols[k], k))
        inverse = root * root
        scale = jnp.where(sub == k, root, scale)
        head = {j: row_of(cols[j], k) for j in range(k + 1, SUB)}
        tail = [row_of(x, k) for x in rows]
        factor = jnp.where(sub > k, cols[k] * inverse, 0.0)
        for j in range(k + 1, SUB):
            cols[j] = cols[j] - factor * head[j]
        rows = [x - factor * y for x, y in zip(rows, tail)]
        inverses.append(inverse)
        heads.append(head)
        tails.append(tail)
    for b in range(width):
        done = rows[b] * scale
        if b == 0:
            done = jnp.where(lane >= sub + r0, done, 0.0)
        out_ref[base + r0 : base + r0 + SUB, base + b * BLK : base + (b + 1) * BLK] = done
    following = None
    for i in range(step + 1, BLK // SUB):
        here = slice(i * SUB, (i + 1) * SUB)
        other = [panel[here, b * BLK : (b + 1) * BLK] for b in range(width)]
        cols = columns(other[0], r0)
        for k in range(SUB):
            factor = cols[k] * inverses[k]
            for j in range(k + 1, SUB):
                cols[j] = cols[j] - factor * heads[k][j]
            other = [x - factor * y for x, y in zip(other, tails[k])]
        if following is None:
            following = other
        else:
            for b in range(width):
                panel[here, b * BLK : (b + 1) * BLK] = other[b]
    return following


def factor_kernel(scaling, g_ref, out_ref, *panels):
    nb = len(panels)
    out_ref[...] = jnp.zeros_like(out_ref)
    offset = 0
    for ib in range(nb):
        for jb in range(nb - ib):
            panels[ib][:, jb * BLK : (jb + 1) * BLK] = g_ref[offset : offset + BLK] * scaling
            offset += BLK
    for ib in range(nb):
        base = ib * BLK
        width = nb - ib
        rows = [panels[ib][0:SUB, b * BLK : (b + 1) * BLK] for b in range(width)]
        for step in range(BLK // SUB):
            rows = eliminate(panels[ib], out_ref, base, step, width, rows)
        for jb in range(ib + 1, nb):
            left = out_ref[base : base + BLK, jb * BLK : (jb + 1) * BLK]
            right = out_ref[base : base + BLK, jb * BLK :]
            panels[jb][...] -= lax.dot_general(
                left,
                right,
                (((0,), (0,)), ((), ())),
                precision=lax.Precision.HIGHEST,
                preferred_element_type=jnp.float32,
            )


def factor(gram, snaps, total_rows):
    nb = snaps // BLK
    return pl.pallas_call(
        functools.partial(factor_kernel, 1.0 / total_rows),
        out_shape=jax.ShapeDtypeStruct((snaps, snaps), jnp.float32),
        in_specs=[pl.BlockSpec(memory_space=pltpu.VMEM)],
        out_specs=pl.BlockSpec(memory_space=pltpu.VMEM),
        scratch_shapes=[pltpu.VMEM((BLK, (nb - ib) * BLK), jnp.float32) for ib in range(nb)],
        compiler_params=pltpu.CompilerParams(vmem_limit_bytes=VMEM_LIMIT),
        name="cholesky_factor",
    )(gram)


def local(n_row, n_tile, cam_disp, footprint, stencil, frac, coef):
    snaps = cam_disp.shape[-1]
    world, cells = footprint.shape[2], coef.shape[-1]
    velocity, gram = velocity_and_gram(cam_disp, footprint, stencil, frac, coef, n_row)
    rfactor = factor(sum_all(gram, n_row, n_tile), snaps, n_row * n_tile * world * 3 * cells)
    return (velocity.reshape(1, 1, world, 3, cells, snaps), rfactor)


def solution(mesh):
    in_specs = (
        P("row", "tile", None, None, None, None),
        P("row", "tile", None, None),
        P("row", "tile", None, None, None, None),
        P("row", "tile", None, None, None, None),
        P("row", "tile", None, None, None, None),
    )
    out_specs = (P("row", "tile", None, None, None, None), P())
    body = functools.partial(local, mesh.shape["row"], mesh.shape["tile"])
    return jax.shard_map(body, mesh=mesh, in_specs=in_specs, out_specs=out_specs, check_vma=False)
```
